128 devices in a mesh: dp: 8 (over x_lo, y), seq: 16 (over x_hi, z, core).
Axes of the slice: x: 4 (x_hi: 2, x_lo: 2; x = x_hi * 2 + x_lo), y: 4, z: 4, core: 2. Of those that a mesh axis runs over, the one named last changes fastest.
Arguments:
- q_time: bfloat16 [8, 16, 256, 16, 128], P('dp', 'seq'), may hold values from -100 to 100
- k_time: bfloat16 [8, 16, 256, 16, 128], P('dp', 'seq'), may hold values from -12 to 12
- v_time: bfloat16 [8, 16, 256, 16, 128], P('dp', 'seq'), may hold values from -6 to 6
- q_space: bfloat16 [8, 16, 256, 16, 128], P('dp', 'seq'), may hold values from -100 to 100
- k_space: bfloat16 [8, 16, 256, 16, 128], P('dp', 'seq'), may hold values from -12 to 12
- audio_now: bfloat16 [8, 1024, 1024], P('dp', 'seq'), may hold values from -6 to 6
- audio_earlier: bfloat16 [8, 1024, 1024], P('dp', 'seq'), may hold values from -6 to 6
- cotangent: bfloat16 [8, 1024, 4096], P('dp', 'seq'), may hold values from -6 to 6
- audio_weight: bfloat16 [1024, 4096], replicated, may hold values from -0.1875 to 0.1875
Outputs:
- mixed: bfloat16 [8, 16, 256, 16, 128], P('dp', 'seq')
- weight_grad: float32 [1024, 4096], P(('dp', 'seq'))
The draws below stay inside these ranges and needn't reach their ends.
All inputs are finite; a program needn't handle non-finite values.
Results may differ from the reference program's by a relative error of at most 0.013.
Values may be sent and summed in bfloat16 or wider, within the bound.
A program may use at most 128 MiB of HBM per device.

```python
import math
import jax
import jax.numpy as jnp
from jax import lax

HEADS = 16
HD = 128
A_DIM = 1024
C = 8
F = 16
S = 256
AUD = 1024
INNER = 2048


def paired(key, lowest, highest):
    dims_all = (C, F, S, HEADS, HD)
    split_one, split_two, split_three, split_four = jax.random.split(key, 4)
    key_rows = jnp.clip(jax.random.normal(split_one, dims_all, jnp.float32), -6.0, 6.0)
    queries = jnp.clip(jax.random.normal(split_two, dims_all, jnp.float32) * 2.0, -12.0, 12.0)
    chosen = jax.random.randint(split_three, (C, F, S, HEADS, 1), 0, 64) == 0
    factor = jax.random.uniform(split_four, (C, F, S, HEADS, 1), jnp.float32, lowest, highest)
    return (jnp.where(chosen, factor * key_rows, queries), key_rows)


def draw_q_time(key, part):
    queries, key_rows = paired(jax.random.fold_in(key, 11), 2.0, 2.5)
    return queries.astype(jnp.bfloat16)


def draw_k_time(key, part):
    queries, key_rows = paired(jax.random.fold_in(key, 11), 2.0, 2.5)
    return key_rows.astype(jnp.bfloat16)


def draw_q_space(key, part):
    queries, key_rows = paired(jax.random.fold_in(key, 12), 2.0, 2.5)
    return queries.astype(jnp.bfloat16)


def draw_k_space(key, part):
    queries, key_rows = paired(jax.random.fold_in(key, 12), 2.0, 2.5)
    return key_rows.astype(jnp.bfloat16)


def spiked(array, key, source, target, blocks, factor):
    def block_of(position):
        return (jnp.arange(array.shape[position]) // (array.shape[position] // blocks)).reshape((-1,) + (1,) * (array.ndim - 1 - position))

    one_side = jax.random.permutation(key, blocks)[block_of(target)]
    second = (block_of(target) + blocks // 2) % blocks
    return jnp.where((block_of(source) == one_side) | (block_of(source) == second), factor * array, array)


def shard_levels(rng, extent, cuts, smallest, high):
    def one(axis_at, blocks):
        heights = jax.random.uniform(jax.random.fold_in(jax.random.fold_in(rng, 6), axis_at), (blocks,), jnp.float32, smallest / len(cuts), high / len(cuts))
        return jnp.repeat(jnp.exp(heights), extent[axis_at] // blocks).reshape((-1,) + (1,) * (len(extent) - axis_at - 1))

    gain = one(*cuts[0])
    for cut in cuts[1:]:
        gain = gain * one(*cut)
    return gain


def normal_values(rng, dims, scale, bound, cuts=(), dtype=jnp.bfloat16):
    gain = shard_levels(rng, dims, cuts, -0.22, 0.18) if cuts else 1.0
    values = jax.random.normal(rng, dims, jnp.float32) * scale * gain
    return jnp.minimum(jnp.maximum(values, -bound), bound).astype(dtype)


def noise_with(own_key, shape, deviation, limit, shards, heavy, held_as=jnp.bfloat16):
    drawn = deviation * jax.random.normal(own_key, shape, jnp.float32)
    if shards:
        drawn = drawn * shard_levels(own_key, shape, shards, -0.22, 0.18)
    return jnp.clip(spiked(drawn, jax.random.fold_in(own_key, 3), *heavy), -limit, limit).astype(held_as)


def setup_inputs(seed: int = 0) -> dict:
    splits = jax.random.split(jax.random.key(seed), 10)
    q_time = draw_q_time(jax.random.fold_in(splits[9], 71), 0)
    k_time = draw_k_time(jax.random.fold_in(splits[9], 71), 0)
    v_time = normal_values(splits[2], (C, F, S, HEADS, HD), 1.0, 6.0, ((0, 8), (1, 16)))
    q_space = draw_q_space(jax.random.fold_in(splits[9], 71), 0)
    k_space = draw_k_space(jax.random.fold_in(splits[9], 71), 0)
    audio_now = normal_values(splits[5], (C, AUD, A_DIM), 1.0, 6.0, ((0, 8), (1, 16)))
    audio_earlier = noise_with(splits[6], (C, AUD, A_DIM), 1.0, 6.0, ((0, 8), (1, 16)), (1, 2, 16, 2.0))
    cotangent = normal_values(splits[7], (C, AUD, 2 * INNER), 1.0, 6.0, ((0, 8), (1, 16)))
    audio_weight = normal_values(splits[8], (A_DIM, 2 * INNER), A_DIM ** -0.5, 0.1875)
    return {"q_time": q_time, "k_time": k_time, "v_time": v_time, "q_space": q_space, "k_space": k_space, "audio_now": audio_now, "audio_earlier": audio_earlier, "cotangent": cotangent, "audio_weight": audio_weight}


def normalize(scores):
    row_max = lax.optimization_barrier(jnp.max(scores, axis=-1, keepdims=True))
    expo = jnp.exp(scores - row_max)
    return (expo / lax.optimization_barrier(jnp.sum(expo, axis=-1, keepdims=True))).astype(jnp.bfloat16)

def reference(q_time, k_time, v_time, q_space, k_space, audio_now, audio_earlier, cotangent, audio_weight):
    factor = 1.0 / math.sqrt(HD)
    f32 = jnp.float32
    audio_kv = jnp.dot(audio_now.reshape(C * AUD, A_DIM), audio_weight, preferred_element_type=f32).astype(jnp.bfloat16)
    audio_kv = audio_kv.reshape(C, AUD, 2, HEADS, HD)

    def temporal(inputs):
        queries, key_rows, values = inputs
        scores = jnp.einsum('fshd,gshd->shfg', queries.astype(f32), key_rows.astype(f32)) * factor
        weights = normalize(scores)
        result = jnp.einsum('shfg,gshd->fshd', weights.astype(f32), values.astype(f32))
        return (values.astype(f32) + result).astype(jnp.bfloat16)
    hidden = lax.map(temporal, (q_time, k_time, v_time))

    def per_frame(inputs):
        queries, key_rows, values, audio_keys, audio_values = inputs
        scores = jnp.einsum('shd,thd->hst', queries.astype(f32), key_rows.astype(f32)) * factor
        spatial = jnp.einsum('hst,thd->shd', normalize(scores).astype(f32), values.astype(f32))
        cross_scores = jnp.einsum('shd,ahd->hsa', queries.astype(f32), audio_keys.astype(f32)) * factor
        cross_mix = jnp.einsum('hsa,ahd->shd', normalize(cross_scores).astype(f32), audio_values.astype(f32))
        return (values.astype(f32) + spatial + cross_mix).astype(jnp.bfloat16)
    audio_keys = jnp.broadcast_to(audio_kv[:, None, :, 0], (C, F, AUD, HEADS, HD)).reshape(C * F, AUD, HEADS, HD)
    audio_values = jnp.broadcast_to(audio_kv[:, None, :, 1], (C, F, AUD, HEADS, HD)).reshape(C * F, AUD, HEADS, HD)
    mixed = lax.map(per_frame, (q_space.reshape(C * F, S, HEADS, HD), k_space.reshape(C * F, S, HEADS, HD), hidden.reshape(C * F, S, HEADS, HD), audio_keys, audio_values))
    mixed = mixed.reshape(C, F, S, HEADS, HD)
    weight_grad = jnp.dot(audio_earlier.reshape(C * AUD, A_DIM).T, cotangent.reshape(C * AUD, 2 * INNER), preferred_element_type=f32)
    return (mixed, weight_grad)
```

```python
import functools
import math

import jax
import jax.numpy as jnp
from jax import lax
from jax.experimental import pallas as pl
from jax.experimental.pallas import tpu as pltpu
from jax.sharding import PartitionSpec as P

MESH = pl.DeviceIdType.MESH
F32 = jnp.float32
BF16 = jnp.bfloat16
HEADS, HD, SPOTS, FRAMES = 16, 128, 256, 16
CHUNKS = 4
PART = SPOTS // FRAMES // CHUNKS
EXP_SCALE = math.log2(math.e) / math.sqrt(HD)
NEG = -1e30


def dot(a, b):
    return lax.dot_general(a, b, (((1,), (0,)), ((), ())), preferred_element_type=F32)


def dot_nt(a, b):
    return lax.dot_general(a, b, (((1,), (1,)), ((), ())), preferred_element_type=F32)


def dot_tn(a, b):
    return lax.dot_general(a, b, (((0,), (0,)), ((), ())), preferred_element_type=F32)


def softmax(scores):
    row_max = jnp.max(scores, axis=-1, keepdims=True)
    expo = jnp.exp2((scores - row_max) * EXP_SCALE)
    return (expo * (1.0 / jnp.sum(expo, axis=-1, keepdims=True))).astype(BF16)


def kernel(
    q_time, k_time, v_time, q_space, k_space, audio_now, audio_earlier, cotangent, weight,
    mixed, grad,
    arrived, back, hidden, q_raw, k_raw, q_heads, k_heads, hid_heads, spatial, cross, out_heads,
    audio, w_vmem, kv, earlier, cotan, part_z, from_z, part_x, from_x, part_y, rows, bias, perm,
    local_sem, qkv_send, qkv_recv, hid_send, hid_recv, aud_send, aud_recv, grad_send, grad_recv,
    out_sem,
):
    dp = lax.axis_index("dp")
    me = lax.axis_index("seq")
    x_lo, y = dp // 4, dp % 4
    x_hi, z, core = me // 8, (me // 2) % 4, me % 2
    x = x_hi * 2 + x_lo
    line = y * 2 + core

    def at(x_, y_, z_, c_):
        return ((x_ % 2) * 4 + y_, (x_ // 2) * 8 + z_ * 2 + c_)

    def send(src, dst, send_sem, recv_sem, device):
        pltpu.make_async_remote_copy(
            src, dst, send_sem, recv_sem, device_id=device, device_id_type=MESH
        ).start()

    def local(src, dst, sem):
        pltpu.make_async_copy(src, dst, sem).start()

    def wait(ref, sem):
        pltpu.make_async_copy(ref, ref, sem).wait()

    def seq_peer(step):
        far = step % 2
        rest = step // 2
        return ((x_hi + far) % 2) * 8 + ((z + rest // 2) % 4) * 2 + (core + rest) % 2

    def y_peer(step):
        return (y + step // 2) % 4, (core + step) % 2

    for c in range(CHUNKS):
        local(q_space.at[:, c], q_raw.at[c], local_sem.at[0])
        local(k_space.at[:, c], k_raw.at[c], local_sem.at[1])
        for t, ref in enumerate((q_time, k_time, v_time)):
            local(ref.at[me, c], arrived.at[c, t, me], qkv_recv.at[c])
    local(weight, w_vmem, local_sem.at[2])
    local(audio_now, audio.at[me // 2, core], local_sem.at[3])
    local(audio_earlier, earlier.at[line], grad_recv.at[0])
    local(cotangent.at[:, pl.ds(pl.multiple_of(line * 512, 512), 512)], cotan.at[line], grad_recv.at[1])

    barrier = pltpu.get_barrier_semaphore()

    def greet(device):
        pl.semaphore_signal(barrier, inc=1, device_id=device, device_id_type=MESH)

    def greet_seq(step, carry):
        greet((dp, seq_peer(step)))
        return carry

    lax.fori_loop(1, 16, greet_seq, 0)

    def greet_y(step, carry):
        y_, c_ = y_peer(step)
        greet(at(x, y_, z, c_))
        return carry

    lax.fori_loop(2, 8, greet_y, 0)
    greet(at((x + 1) % 4, y, z, core))
    greet(at((x + 3) % 4, y, z, core))
    pl.semaphore_wait(barrier, 23)

    mine = audio.at[me // 2, core]
    send(audio_now, mine, aud_send.at[0], aud_recv.at[0], at((x + 2) % 4, y, z, core))
    for d in (1, 3, 2):
        send(audio_now, mine, aud_send.at[0], aud_recv.at[1], at(x, y, (z + d) % 4, core))

    def send_qkv(c):
        def body(step, carry):
            peer = seq_peer(step)
            for t, ref in enumerate((q_time, k_time, v_time)):
                send(ref.at[peer, c], arrived.at[c, t, me], qkv_send.at[t], qkv_recv.at[c], (dp, peer))
            return carry

        lax.fori_loop(1, 16, body, 0)

    send_qkv(0)

    def send_y(step, carry):
        y_, c_ = y_peer(step)
        to = at(x, y_, z, c_)
        cols = pl.ds(pl.multiple_of((y_ * 2 + c_) * 512, 512), 512)
        send(audio_earlier, earlier.at[line], grad_send.at[0], grad_recv.at[0], to)
        send(cotangent.at[:, cols], cotan.at[line], grad_send.at[1], grad_recv.at[1], to)
        return carry

    lax.fori_loop(1, 8, send_y, 0)
    for c in range(1, CHUNKS):
        send_qkv(c)

    row = lax.broadcasted_iota(jnp.int32, (256, 256), 0)
    col = lax.broadcasted_iota(jnp.int32, (256, 256), 1)
    bias[...] = jnp.where(row % 16 == col % 16, 0.0, NEG).astype(F32)
    perm[...] = jnp.where(col == (row % 16) * 16 + row // 16, 1.0, 0.0).astype(BF16)

    def to_heads(src, dst, first, count):
        def body(i, carry):
            block = src[i // 4, pl.ds((i % 4) * (16 // PART), 16 // PART)].reshape(256, HD)
            turned = dot(perm[...], block).astype(BF16).reshape(HEADS, 16, HD)
            dst[:, pl.ds(pl.multiple_of(i * 16, 16), 16), :] = turned
            return carry

        lax.fori_loop(first, first + count, body, 0)

    wait(q_raw, local_sem.at[0])
    to_heads(q_raw, q_heads, 0, 16)
    wait(k_raw, local_sem.at[1])
    to_heads(k_raw, k_heads, 0, 16)

    wait(mine, aud_recv.at[0])
    other = ((x_hi + 1) % 2) * 4 + z
    theirs = audio.at[other, core]
    for d in (1, 3, 2):
        send(theirs, theirs, aud_send.at[0], aud_recv.at[1], at(x, y, (z + d) % 4, core))

    def spatial_scores(h, carry):
        spatial[h] = softmax(dot_nt(q_heads[h], k_heads[h]))
        return carry

    lax.fori_loop(0, HEADS, spatial_scores, 0)

    wait(earlier, grad_recv.at[0])
    wait(cotan, grad_recv.at[1])

    def partial_rows(i, carry):
        x_lo_, y_ = i // 4, i % 4
        lanes = pl.ds(pl.multiple_of(i * 128, 128), 128)
        block = dot_tn(earlier[:, :, lanes].reshape(512, 128), cotan[...].reshape(512, 512))
        block = block.astype(BF16).reshape(2, 4, 16, 512)
        for a in range(2):
            for b in range(4):
                part_z[b, a * 2 + x_lo_, y_] = block[a, b]
        return carry

    lax.fori_loop(0, 8, partial_rows, 0)
    for d in (1, 3, 2):
        z_ = (z + d) % 4
        send(part_z.at[z_], from_z.at[z], grad_send.at[2], grad_recv.at[2], at(x, y, z_, core))
    local(part_z.at[z], from_z.at[z], grad_recv.at[2])

    wait(audio_now, local_sem.at[3])
    wait(audio.at[pl.ds(0, 6), 0], aud_recv.at[1])
    side = audio.at[:, core]
    send(side, side, aud_send.at[1], aud_recv.at[2], at(x, y, z, 1 - core))

    def temporal(c):
        wait(arrived.at[c], qkv_recv.at[c])

        def body(s, carry):
            queries = arrived[c, 0, :, s].reshape(256, HD)
            key_rows = arrived[c, 1, :, s].reshape(256, HD)
            values = arrived[c, 2, :, s].reshape(256, HD)
            weights = softmax(dot_nt(queries, key_rows) + bias[...])
            result = values.astype(F32) + dot(weights, values)
            back[c, :, s] = result.astype(BF16).reshape(FRAMES, HEADS, HD)
            return carry

        lax.fori_loop(0, PART, body, 0)

        def go(step, carry):
            peer = seq_peer(step)
            send(back.at[c, peer], hidden.at[c, me], hid_send.at[0], hid_recv.at[c], (dp, peer))
            return carry

        lax.fori_loop(1, 16, go, 0)
        local(back.at[c, me], hidden.at[c, me], hid_recv.at[c])

    def audio_pair(p, carry):
        tokens = audio[...].reshape(1024, 1024)
        lanes = pl.ds(pl.multiple_of(p * 256, 256), 256)
        more = pl.ds(pl.multiple_of(2048 + p * 256, 256), 256)
        kv[0] = dot(tokens, w_vmem[:, lanes]).astype(BF16)
        kv[1] = dot(tokens, w_vmem[:, more]).astype(BF16)
        for i in range(2):
            span = slice(i * 128, (i + 1) * 128)
            weights = softmax(dot_nt(q_heads[p * 2 + i], kv[0, :, span]))
            cross[p * 2 + i] = dot(weights, kv[1, :, span])
        return carry

    wait(w_vmem, local_sem.at[2])
    wait(audio.at[:, 0], aud_recv.at[2])
    lax.fori_loop(0, 2, audio_pair, 0)
    temporal(0)
    lax.fori_loop(2, 4, audio_pair, 0)

    wait(from_z, grad_recv.at[2])
    for x_ in range(4):
        total = from_z[0, x_].astype(F32)
        for z_ in range(1, 4):
            total += from_z[z_, x_].astype(F32)
        part_x[x_] = total.astype(BF16)
    for d in (2, 1, 3):
        x_ = (x + d) % 4
        send(part_x.at[x_], from_x.at[x], grad_send.at[3], grad_recv.at[3], at(x_, y, z, core))
    local(part_x.at[x], from_x.at[x], grad_recv.at[3])

    temporal(1)
    lax.fori_loop(4, 6, audio_pair, 0)
    temporal(2)
    lax.fori_loop(6, 8, audio_pair, 0)

    wait(from_x, grad_recv.at[3])
    for y_ in range(4):
        total = from_x[0, y_].astype(F32)
        for x_ in range(1, 4):
            total += from_x[x_, y_].astype(F32)
        part_y[y_] = total.reshape(2, 8, 512)
    cols = pl.ds(pl.multiple_of(line * 512, 512), 512)

    def send_rows(step, carry):
        y_, c_ = y_peer(step)
        send(part_y.at[y_, c_], rows.at[:, cols], grad_send.at[4], grad_recv.at[4], at(x, y_, z, c_))
        return carry

    lax.fori_loop(1, 8, send_rows, 0)
    local(part_y.at[y, core], rows.at[:, cols], grad_recv.at[4])

    temporal(3)

    wait(rows, grad_recv.at[4])
    local(rows, grad, out_sem.at[1])

    for c in range(CHUNKS):
        wait(hidden.at[c], hid_recv.at[c])
        to_heads(hidden, hid_heads, c * 4, 4)

    def finish(h, carry):
        values = hid_heads[h]
        result = values.astype(F32) + dot(spatial[h], values) + cross[h]
        out_heads[h] = result.astype(BF16)
        local(out_heads.at[h], mixed.at[h], out_sem.at[0])
        return carry

    lax.fori_loop(0, HEADS, finish, 0)

    wait(mixed, out_sem.at[0])
    wait(grad, out_sem.at[1])
    for t, ref in enumerate((q_time, k_time, v_time)):
        wait(ref.at[pl.ds(0, 15)], qkv_send.at[t])
    wait(back.at[:, pl.ds(0, 15)], hid_send.at[0])
    wait(audio.at[pl.ds(0, 7), 0], aud_send.at[0])
    wait(audio.at[:, 0], aud_send.at[1])
    wait(earlier.at[pl.ds(0, 7)], grad_send.at[0])
    wait(cotan.at[pl.ds(0, 7)], grad_send.at[1])
    wait(from_z.at[pl.ds(0, 3)], grad_send.at[2])
    wait(from_x.at[pl.ds(0, 3)], grad_send.at[3])
    wait(rows.at[:, pl.ds(0, 7 * 512)], grad_send.at[4])


def local(
    q_time, k_time, v_time, q_space, k_space, audio_now, audio_earlier, cotangent, audio_weight
):
    split = (FRAMES, CHUNKS, PART, HEADS, HD)
    vmem = lambda shape, dtype: pltpu.VMEM(shape, dtype)
    dma = lambda n: pltpu.SemaphoreType.DMA((n,))
    anywhere = pl.BlockSpec(memory_space=pl.ANY)
    mixed, grad = pl.pallas_call(
        kernel,
        out_shape=(
            jax.ShapeDtypeStruct((HEADS, SPOTS, HD), BF16),
            jax.ShapeDtypeStruct((8, 4096), F32),
        ),
        in_specs=[anywhere] * 9,
        out_specs=(anywhere, anywhere),
        scratch_shapes=[
            vmem((CHUNKS, 3, FRAMES, PART, HEADS, HD), BF16),
            vmem((CHUNKS, FRAMES, PART, HEADS, HD), BF16),
            vmem((CHUNKS, FRAMES, PART, HEADS, HD), BF16),
            vmem((CHUNKS, FRAMES, PART, HEADS, HD), BF16),
            vmem((CHUNKS, FRAMES, PART, HEADS, HD), BF16),
            vmem((HEADS, SPOTS, HD), BF16),
            vmem((HEADS, SPOTS, HD), BF16),
            vmem((HEADS, SPOTS, HD), BF16),
            vmem((HEADS, SPOTS, SPOTS), BF16),
            vmem((HEADS, SPOTS, HD), F32),
            vmem((HEADS, SPOTS, HD), BF16),
            vmem((8, 2, 64, 1024), BF16),
            vmem((1024, 4096), BF16),
            vmem((2, 1024, 256), BF16),
            vmem((8, 64, 1024), BF16),
            vmem((8, 64, 512), BF16),
            vmem((4, 4, 4, 16, 512), BF16),
            vmem((4, 4, 4, 16, 512), BF16),
            vmem((4, 4, 16, 512), BF16),
            vmem((4, 4, 16, 512), BF16),
            vmem((4, 2, 8, 512), F32),
            vmem((8, 4096), F32),
            vmem((256, 256), F32),
            vmem((256, 256), BF16),
            dma(4), dma(3), dma(CHUNKS), dma(1), dma(CHUNKS), dma(2), dma(3), dma(5), dma(5), dma(2),
        ],
        compiler_params=pltpu.CompilerParams(
            collective_id=0, has_side_effects=True, vmem_limit_bytes=52 * 2**20
        ),
        name="block",
    )(
        q_time.reshape(split), k_time.reshape(split), v_time.reshape(split),
        q_space.reshape(split), k_space.reshape(split),
        audio_now[0], audio_earlier[0], cotangent[0], audio_weight,
    )
    mixed = mixed.reshape(HEADS, CHUNKS, FRAMES, PART, HD).transpose(2, 1, 3, 0, 4)
    return mixed.reshape(1, 1, SPOTS, HEADS, HD), grad


def solution(mesh):
    placed = (
        P("dp", "seq", None, None, None),
        P("dp", "seq", None, None, None),
        P("dp", "seq", None, None, None),
        P("dp", "seq", None, None, None),
        P("dp", "seq", None, None, None),
        P("dp", "seq", None),
        P("dp", "seq", None),
        P("dp", "seq", None),
        P(),
    )
    return jax.shard_map(
        local,
        mesh=mesh,
        in_specs=placed,
        out_specs=(P("dp", "seq", None, None, None), P(("dp", "seq"), None)),
        check_vma=False,
    )
```

```python
import functools
import math

import jax
import jax.numpy as jnp
from jax import lax
from jax.experimental import pallas as pl
from jax.experimental.pallas import tpu as pltpu
from jax.sharding import PartitionSpec as P

MESH = pl.DeviceIdType.MESH
F32 = jnp.float32
BF16 = jnp.bfloat16
HEADS, HD, SPOTS, FRAMES = 16, 128, 256, 16
CHUNKS = 4
PART = SPOTS // FRAMES // CHUNKS
EXP_SCALE = math.log2(math.e) / math.sqrt(HD)
NEG = -1e30


def dot(a, b):
    return lax.dot_general(a, b, (((1,), (0,)), ((), ())), preferred_element_type=F32)


def dot_nt(a, b):
    return lax.dot_general(a, b, (((1,), (1,)), ((), ())), preferred_element_type=F32)


def dot_tn(a, b):
    return lax.dot_general(a, b, (((0,), (0,)), ((), ())), preferred_element_type=F32)


def softmax(scores):
    row_max = jnp.max(scores, axis=-1, keepdims=True)
    expo = jnp.exp2((scores - row_max) * EXP_SCALE)
    return expo, jnp.sum(expo, axis=-1, keepdims=True)


def kernel(
    q_time, k_time, v_time, q_space, k_space, audio_now, audio_earlier, cotangent, weight,
    mixed, grad,
    arrived, back, hidden, q_raw, k_raw, q_heads, k_heads, hid_heads, spatial, cross, out_heads,
    audio, w_vmem, kv, earlier, cotan, part_x, from_x, part_z, from_z, part_y, rows, bias, perm,
    local_sem, qkv_send, qkv_recv, hid_send, hid_recv, aud_send, aud_recv, grad_send, grad_recv,
    out_sem,
):
    dp = lax.axis_index("dp")
    me = lax.axis_index("seq")
    x_lo, y = dp // 4, dp % 4
    x_hi, z, core = me // 8, (me // 2) % 4, me % 2
    x = x_hi * 2 + x_lo
    line = y * 2 + core

    def at(x_, y_, z_, c_):
        return ((x_ % 2) * 4 + y_, (x_ // 2) * 8 + z_ * 2 + c_)

    def send(src, dst, send_sem, recv_sem, device):
        pltpu.make_async_remote_copy(
            src, dst, send_sem, recv_sem, device_id=device, device_id_type=MESH
        ).start()

    def local(src, dst, sem):
        pltpu.make_async_copy(src, dst, sem).start()

    def wait(ref, sem):
        pltpu.make_async_copy(ref, ref, sem).wait()

    def seq_peer(step):
        far = step % 2
        rest = step // 2
        return ((x_hi + far) % 2) * 8 + ((z + rest // 2) % 4) * 2 + (core + rest) % 2

    def y_peer(step):
        return (y + step // 2) % 4, (core + step) % 2

    for c in range(CHUNKS):
        local(q_space.at[:, c], q_raw.at[c], local_sem.at[0])
        local(k_space.at[:, c], k_raw.at[c], local_sem.at[1])
        for t, ref in enumerate((q_time, k_time, v_time)):
            local(ref.at[me, c], arrived.at[c, t, me], qkv_recv.at[c])
    local(weight, w_vmem, local_sem.at[2])
    local(audio_now, audio.at[me // 2, core], local_sem.at[3])
    local(audio_earlier, earlier.at[line], grad_recv.at[0])
    local(cotangent.at[:, pl.ds(pl.multiple_of(line * 512, 512), 512)], cotan.at[line], grad_recv.at[1])

    barrier = pltpu.get_barrier_semaphore()

    def greet(device):
        pl.semaphore_signal(barrier, inc=1, device_id=device, device_id_type=MESH)

    def greet_seq(step, carry):
        greet((dp, seq_peer(step)))
        return carry

    lax.fori_loop(1, 16, greet_seq, 0)

    def greet_y(step, carry):
        y_, c_ = y_peer(step)
        greet(at(x, y_, z, c_))
        return carry

    lax.fori_loop(2, 8, greet_y, 0)
    greet(at((x + 1) % 4, y, z, core))
    greet(at((x + 3) % 4, y, z, core))
    pl.semaphore_wait(barrier, 23)

    mine = audio.at[me // 2, core]
    send(audio_now, mine, aud_send.at[0], aud_recv.at[0], at((x + 2) % 4, y, z, core))
    for d in (1, 3, 2):
        send(audio_now, mine, aud_send.at[0], aud_recv.at[1], at(x, y, (z + d) % 4, core))

    def send_qkv(c):
        def body(step, carry):
            peer = seq_peer(step)
            for t, ref in enumerate((q_time, k_time, v_time)):
                send(ref.at[peer, c], arrived.at[c, t, me], qkv_send.at[t], qkv_recv.at[c], (dp, peer))
            return carry

        lax.fori_loop(1, 16, body, 0)

    send_qkv(0)

    def send_y(step, carry):
        y_, c_ = y_peer(step)
        to = at(x, y_, z, c_)
        cols = pl.ds(pl.multiple_of((y_ * 2 + c_) * 512, 512), 512)
        send(audio_earlier, earlier.at[line], grad_send.at[0], grad_recv.at[0], to)
        send(cotangent.at[:, cols], cotan.at[line], grad_send.at[1], grad_recv.at[1], to)
        return carry

    lax.fori_loop(1, 8, send_y, 0)

    row = lax.broadcasted_iota(jnp.int32, (256, 256), 0)
    col = lax.broadcasted_iota(jnp.int32, (256, 256), 1)
    bias[...] = jnp.where(row % 16 == col % 16, 0.0, NEG).astype(F32)
    perm[...] = jnp.where(col == (row % 16) * 16 + row // 16, 1.0, 0.0).astype(BF16)

    def to_heads(src, dst, c):
        blocks = jnp.concatenate(
            [src[c, pl.ds(i * (16 // PART), 16 // PART)].reshape(256, HD) for i in range(4)], axis=1
        )
        turned = dot(perm[...], blocks).astype(BF16)
        for i in range(4):
            dst[:, pl.ds(pl.multiple_of(c * 64 + i * 16, 16), 16), :] = turned[
                :, i * HD : (i + 1) * HD
            ].reshape(HEADS, 16, HD)

    def q_to_heads(c, carry):
        to_heads(q_raw, q_heads, c)
        return carry

    def k_to_heads(c, carry):
        to_heads(k_raw, k_heads, c)
        return carry

    wait(q_raw, local_sem.at[0])
    lax.fori_loop(0, CHUNKS, q_to_heads, 0)
    wait(k_raw, local_sem.at[1])
    lax.fori_loop(0, CHUNKS, k_to_heads, 0)

    wait(mine, aud_recv.at[0])
    other = ((x_hi + 1) % 2) * 4 + z
    theirs = audio.at[other, core]
    for d in (1, 3, 2):
        send(theirs, theirs, aud_send.at[0], aud_recv.at[1], at(x, y, (z + d) % 4, core))
    send_qkv(1)

    def spatial_scores(i, carry):
        for h in (2 * i, 2 * i + 1):
            expo, total = softmax(dot_nt(q_heads[h], k_heads[h]))
            spatial[h] = (expo * (1.0 / total)).astype(BF16)
        return carry

    lax.fori_loop(0, HEADS // 2, spatial_scores, 0)

    def temporal(c):
        wait(arrived.at[c], qkv_recv.at[c])

        def attend(i, carry):
            for s in (2 * i, 2 * i + 1):
                queries = arrived[c, 0, :, s].reshape(256, HD)
                key_rows = arrived[c, 1, :, s].reshape(256, HD)
                values = arrived[c, 2, :, s].reshape(256, HD)
                expo, total = softmax(dot_nt(queries, key_rows) + bias[...])
                result = values.astype(F32) + dot(expo.astype(BF16), values) * (1.0 / total)
                back[c, :, s] = result.astype(BF16).reshape(FRAMES, HEADS, HD)
            return carry

        lax.fori_loop(0, PART // 2, attend, 0)

        def go(step, carry):
            peer = seq_peer(step)
            send(back.at[c, peer], hidden.at[c, me], hid_send.at[0], hid_recv.at[c], (dp, peer))
            return carry

        lax.fori_loop(1, 16, go, 0)
        local(back.at[c, me], hidden.at[c, me], hid_recv.at[c])

    temporal(0)

    wait(earlier, grad_recv.at[0])
    wait(cotan, grad_recv.at[1])

    def partial_rows(i, carry):
        x_lo_, y_ = i // 4, i % 4
        lanes = pl.ds(pl.multiple_of(i * 128, 128), 128)
        block = dot_tn(earlier[:, :, lanes].reshape(512, 128), cotan[...].reshape(512, 512))
        block = block.astype(BF16).reshape(2, 4, 16, 512)
        for a in range(2):
            for b in range(4):
                part_x[a * 2 + x_lo_, b, y_] = block[a, b]
        return carry

    lax.fori_loop(0, 8, partial_rows, 0)
    for d in (2, 1, 3):
        x_ = (x + d) % 4
        send(part_x.at[x_], from_x.at[x], grad_send.at[2], grad_recv.at[2], at(x_, y, z, core))
    local(part_x.at[x], from_x.at[x], grad_recv.at[2])
    send_qkv(2)

    wait(audio_now, local_sem.at[3])
    wait(audio.at[pl.ds(0, 6), 0], aud_recv.at[1])
    side = audio.at[:, core]
    send(side, side, aud_send.at[1], aud_recv.at[2], at(x, y, z, 1 - core))

    temporal(1)
    send_qkv(3)

    def audio_pair(p, carry):
        tokens = audio[...].reshape(1024, 1024)
        lanes = pl.ds(pl.multiple_of(p * 256, 256), 256)
        more = pl.ds(pl.multiple_of(2048 + p * 256, 256), 256)
        kv[0] = dot(tokens, w_vmem[:, lanes]).astype(BF16)
        kv[1] = dot(tokens, w_vmem[:, more]).astype(BF16)
        for i in range(2):
            span = slice(i * 128, (i + 1) * 128)
            expo, total = softmax(dot_nt(q_heads[p * 2 + i], kv[0, :, span]))
            cross[p * 2 + i] = dot(expo.astype(BF16), kv[1, :, span]) * (1.0 / total)
        return carry

    wait(w_vmem, local_sem.at[2])
    wait(audio.at[:, 0], aud_recv.at[2])
    lax.fori_loop(0, 4, audio_pair, 0)
    temporal(2)

    wait(from_x, grad_recv.at[2])
    for z_ in range(4):
        total = from_x[0, z_].astype(F32)
        for x_ in range(1, 4):
            total += from_x[x_, z_].astype(F32)
        part_z[z_] = total.astype(BF16)
    for d in (1, 3, 2):
        z_ = (z + d) % 4
        send(part_z.at[z_], from_z.at[z], grad_send.at[3], grad_recv.at[3], at(x, y, z_, core))
    local(part_z.at[z], from_z.at[z], grad_recv.at[3])

    lax.fori_loop(4, 8, audio_pair, 0)
    temporal(3)

    wait(from_z, grad_recv.at[3])
    for y_ in range(4):
        total = from_z[0, y_].astype(F32)
        for z_ in range(1, 4):
            total += from_z[z_, y_].astype(F32)
        part_y[y_] = total.reshape(2, 8, 512)
    cols = pl.ds(pl.multiple_of(line * 512, 512), 512)

    def send_rows(step, carry):
        y_, c_ = y_peer(step)
        send(part_y.at[y_, c_], rows.at[:, cols], grad_send.at[4], grad_recv.at[4], at(x, y_, z, c_))
        return carry

    lax.fori_loop(1, 8, send_rows, 0)
    local(part_y.at[y, core], rows.at[:, cols], grad_recv.at[4])

    for c in range(CHUNKS):
        wait(hidden.at[c], hid_recv.at[c])
        to_heads(hidden, hid_heads, c)

    def finish(i, carry):
        for h in [4 * i + j for j in range(4)]:
            values = hid_heads[h]
            result = values.astype(F32) + dot(spatial[h], values) + cross[h]
            out_heads[h] = result.astype(BF16)
            local(out_heads.at[h], mixed.at[h], out_sem.at[0])
        return carry

    lax.fori_loop(0, HEADS // 4, finish, 0)
    wait(rows, grad_recv.at[4])
    local(rows, grad, out_sem.at[1])

    wait(mixed, out_sem.at[0])
    wait(grad, out_sem.at[1])
    for t, ref in enumerate((q_time, k_time, v_time)):
        wait(ref.at[pl.ds(0, 15)], qkv_send.at[t])
    wait(back.at[:, pl.ds(0, 15)], hid_send.at[0])
    wait(audio.at[pl.ds(0, 7), 0], aud_send.at[0])
    wait(audio.at[:, 0], aud_send.at[1])
    wait(earlier.at[pl.ds(0, 7)], grad_send.at[0])
    wait(cotan.at[pl.ds(0, 7)], grad_send.at[1])
    wait(from_x.at[pl.ds(0, 3)], grad_send.at[2])
    wait(from_z.at[pl.ds(0, 3)], grad_send.at[3])
    wait(rows.at[:, pl.ds(0, 7 * 512)], grad_send.at[4])


def local(
    q_time, k_time, v_time, q_space, k_space, audio_now, audio_earlier, cotangent, audio_weight
):
    split = (FRAMES, CHUNKS, PART, HEADS, HD)
    vmem = lambda shape, dtype: pltpu.VMEM(shape, dtype)
    dma = lambda n: pltpu.SemaphoreType.DMA((n,))
    anywhere = pl.BlockSpec(memory_space=pl.ANY)
    mixed, grad = pl.pallas_call(
        kernel,
        out_shape=(
            jax.ShapeDtypeStruct((HEADS, SPOTS, HD), BF16),
            jax.ShapeDtypeStruct((8, 4096), F32),
        ),
        in_specs=[anywhere] * 9,
        out_specs=(anywhere, anywhere),
        scratch_shapes=[
            vmem((CHUNKS, 3, FRAMES, PART, HEADS, HD), BF16),
            vmem((CHUNKS, FRAMES, PART, HEADS, HD), BF16),
            vmem((CHUNKS, FRAMES, PART, HEADS, HD), BF16),
            vmem((CHUNKS, FRAMES, PART, HEADS, HD), BF16),
            vmem((CHUNKS, FRAMES, PART, HEADS, HD), BF16),
            vmem((HEADS, SPOTS, HD), BF16),
            vmem((HEADS, SPOTS, HD), BF16),
            vmem((HEADS, SPOTS, HD), BF16),
            vmem((HEADS, SPOTS, SPOTS), BF16),
            vmem((HEADS, SPOTS, HD), F32),
            vmem((HEADS, SPOTS, HD), BF16),
            vmem((8, 2, 64, 1024), BF16),
            vmem((1024, 4096), BF16),
            vmem((2, 1024, 256), BF16),
            vmem((8, 64, 1024), BF16),
            vmem((8, 64, 512), BF16),
            vmem((4, 4, 4, 16, 512), BF16),
            vmem((4, 4, 4, 16, 512), BF16),
            vmem((4, 4, 16, 512), BF16),
            vmem((4, 4, 16, 512), BF16),
            vmem((4, 2, 8, 512), F32),
            vmem((8, 4096), F32),
            vmem((256, 256), F32),
            vmem((256, 256), BF16),
            dma(4), dma(3), dma(CHUNKS), dma(1), dma(CHUNKS), dma(2), dma(3), dma(5), dma(5), dma(2),
        ],
        compiler_params=pltpu.CompilerParams(
            collective_id=0, has_side_effects=True, vmem_limit_bytes=62 * 2**20
        ),
        name="block",
    )(
        q_time.reshape(split), k_time.reshape(split), v_time.reshape(split),
        q_space.reshape(split), k_space.reshape(split),
        audio_now[0], audio_earlier[0], cotangent[0], audio_weight,
    )
    mixed = mixed.reshape(HEADS, CHUNKS, FRAMES, PART, HD).transpose(2, 1, 3, 0, 4)
    return mixed.reshape(1, 1, SPOTS, HEADS, HD), grad


def solution(mesh):
    placed = (
        P("dp", "seq", None, None, None),
        P("dp", "seq", None, None, None),
        P("dp", "seq", None, None, None),
        P("dp", "seq", None, None, None),
        P("dp", "seq", None, None, None),
        P("dp", "seq", None),
        P("dp", "seq", None),
        P("dp", "seq", None),
        P(),
    )
    return jax.shard_map(
        local,
        mesh=mesh,
        in_specs=placed,
        out_specs=(P("dp", "seq", None, None, None), P(("dp", "seq"), None)),
        check_vma=False,
    )
```

```python
import functools
import math

import jax
import jax.numpy as jnp
from jax import lax
from jax.experimental import pallas as pl
from jax.experimental.pallas import tpu as pltpu
from jax.sharding import PartitionSpec as P

MESH = pl.DeviceIdType.MESH
F32 = jnp.float32
BF16 = jnp.bfloat16
HEADS, HD, SPOTS, FRAMES = 16, 128, 256, 16
CHUNKS = 4
PART = SPOTS // FRAMES // CHUNKS
EXP_SCALE = math.log2(math.e) / math.sqrt(HD)
NEG = -1e30
LIMIT = 52 * 2**20


def dot(a, b):
    return lax.dot_general(a, b, (((1,), (0,)), ((), ())), preferred_element_type=F32)


def dot_nt(a, b):
    return lax.dot_general(a, b, (((1,), (1,)), ((), ())), preferred_element_type=F32)


def dot_tn(a, b):
    return lax.dot_general(a, b, (((0,), (0,)), ((), ())), preferred_element_type=F32)


def softmax(scores):
    row_max = jnp.max(scores, axis=-1, keepdims=True)
    expo = jnp.exp2((scores - row_max) * EXP_SCALE)
    return expo, jnp.sum(expo, axis=-1, keepdims=True)


def kernel(
    q_time, k_time, v_time, q_space, k_space, audio_now, audio_earlier, cotangent, weight,
    out_heads, rows_out,
    arrived, back, hidden, q_raw, k_raw, q_heads, k_heads, hid_heads, spatial, cross,
    audio, w_vmem, kv, earlier, cotan, part_x, relay, merged, from_x, part_z, from_z, part_y, rows, bias, perm,
    local_sem, qkv_send, qkv_recv, hid_send, hid_recv, aud_send, aud_recv, grad_send, grad_recv,
):
    dp = lax.axis_index("dp")
    me = lax.axis_index("seq")
    x_lo, y = dp // 4, dp % 4
    x_hi, z, core = me // 8, (me // 2) % 4, me % 2
    x = x_hi * 2 + x_lo
    line = y * 2 + core

    def at(x_, y_, z_, c_):
        return ((x_ % 2) * 4 + y_, (x_ // 2) * 8 + z_ * 2 + c_)

    def send(src, dst, send_sem, recv_sem, device):
        pltpu.make_async_remote_copy(
            src, dst, send_sem, recv_sem, device_id=device, device_id_type=MESH
        ).start()

    def local(src, dst, sem):
        pltpu.make_async_copy(src, dst, sem).start()

    def wait(ref, sem):
        pltpu.make_async_copy(ref, ref, sem).wait()

    def seq_peer(step):
        pure = 1 - (step + 14) // 16
        last = step // 14
        mid = 1 - pure - last
        far = pure + mid * (step % 2)
        along = mid * (1 + (step // 2 + 2) % 3)
        swap = pure * (step % 2) + mid * ((step + 4) // 6 % 2) + last
        return ((x_hi + far) % 2) * 8 + ((z + along) % 4) * 2 + (core + swap) % 2

    def y_peer(step):
        return (y + step // 2) % 4, (core + step) % 2

    barrier = pltpu.get_barrier_semaphore()

    def greet(device):
        pl.semaphore_signal(barrier, inc=1, device_id=device, device_id_type=MESH)

    def greet_seq(step, carry):
        greet((dp, seq_peer(step)))
        return carry

    lax.fori_loop(0, 15, greet_seq, 0)

    def greet_y(step, carry):
        y_, c_ = y_peer(step)
        greet(at(x, y_, z, c_))
        return carry

    lax.fori_loop(2, 8, greet_y, 0)
    greet(at((x + 1) % 4, y, z, core))
    greet(at((x + 3) % 4, y, z, core))
    for c in range(CHUNKS):
        local(q_space.at[:, c], q_raw.at[c], local_sem.at[0])
        local(k_space.at[:, c], k_raw.at[c], local_sem.at[1])
        for t, ref in enumerate((q_time, k_time, v_time)):
            local(ref.at[me, c], arrived.at[c, t, me], qkv_recv.at[c])
    local(weight, w_vmem, local_sem.at[2])
    local(audio_now, audio.at[me // 2, core], local_sem.at[3])
    local(audio_earlier, earlier.at[y, core], grad_recv.at[0])
    local(cotangent.at[:, pl.ds(pl.multiple_of(line * 512, 512), 512)], cotan.at[line], grad_recv.at[1])

    pl.semaphore_wait(barrier, 23)

    mine = audio.at[me // 2, core]
    send(audio_now, mine, aud_send.at[0], aud_recv.at[0], at((x + 2) % 4, y, z, core))
    for d in (1, 3, 2):
        send(audio_now, mine, aud_send.at[0], aud_recv.at[1], at(x, y, (z + d) % 4, core))

    def send_qkv(c, steps):
        def one(peer):
            for t, ref in enumerate((q_time, k_time, v_time)):
                send(ref.at[peer, c], arrived.at[c, t, me], qkv_send.at[t], qkv_recv.at[c], (dp, peer))

        def body(step, carry):
            one(seq_peer(step))
            return carry

        lax.fori_loop(steps[0], steps[1], body, 0)

    send_qkv(0, (0, 2))
    send_qkv(1, (0, 2))
    def send_y(step, carry):
        y_, c_ = y_peer(step)
        to = at(x, y_, z, c_)
        cols = pl.ds(pl.multiple_of((y_ * 2 + c_) * 512, 512), 512)
        send(cotangent.at[:, cols], cotan.at[line], grad_send.at[1], grad_recv.at[1], to)
        return carry

    for d in (1, 3, 2):
        send(audio_earlier, earlier.at[y, core], grad_send.at[0], grad_recv.at[0], at(x, (y + d) % 4, z, core))
    lax.fori_loop(1, 8, send_y, 0)

    row = lax.broadcasted_iota(jnp.int32, (256, 256), 0)
    col = lax.broadcasted_iota(jnp.int32, (256, 256), 1)
    bias[...] = jnp.where(row % 16 == col % 16, 0.0, NEG).astype(F32)
    perm[...] = permutation()

    def to_heads(src, dst, c):
        blocks = jnp.concatenate(
            [src[c, pl.ds(i * (16 // PART), 16 // PART)].reshape(256, HD) for i in range(4)], axis=1
        )
        turned = dot(perm[...], blocks).astype(BF16)
        for i in range(4):
            dst[:, pl.ds(pl.multiple_of(c * 64 + i * 16, 16), 16), :] = turned[
                :, i * HD : (i + 1) * HD
            ].reshape(HEADS, 16, HD)

    def q_to_heads(c, carry):
        to_heads(q_raw, q_heads, c)
        return carry

    def k_to_heads(c, carry):
        to_heads(k_raw, k_heads, c)
        return carry

    def spatial_scores(i, carry):
        for h in (2 * i, 2 * i + 1):
            expo, total = softmax(dot_nt(q_heads[h], k_heads[h]))
            spatial[h] = (expo * (1.0 / total)).astype(BF16)
        return carry

    def temporal(c):
        wait(arrived.at[c], qkv_recv.at[c])

        def attend(i, carry):
            for s in (2 * i, 2 * i + 1):
                queries = arrived[c, 0, :, s].reshape(256, HD)
                key_rows = arrived[c, 1, :, s].reshape(256, HD)
                values = arrived[c, 2, :, s].reshape(256, HD)
                expo, total = softmax(dot_nt(queries, key_rows) + bias[...])
                result = values.astype(F32) + dot(expo.astype(BF16), values) * (1.0 / total)
                back[c, :, s] = result.astype(BF16).reshape(FRAMES, HEADS, HD)
            return carry

        lax.fori_loop(0, PART // 2, attend, 0)

        def go(step, carry):
            peer = seq_peer(step)
            send(back.at[c, peer], hidden.at[c, me], hid_send.at[0], hid_recv.at[c], (dp, peer))
            return carry

        lax.fori_loop(0, 15, go, 0)
        local(back.at[c, me], hidden.at[c, me], hid_recv.at[c])

    def partial_rows(i, carry):
        x_lo_, y_ = i // 4, i % 4
        lanes = pl.ds(pl.multiple_of(i * 128, 128), 128)
        block = dot_tn(earlier[:, :, :, lanes].reshape(512, 128), cotan[...].reshape(512, 512))
        block = block.astype(BF16).reshape(2, 4, 16, 512)
        for a in range(2):
            for b in range(4):
                part_x[a * 2 + x_lo_, b, y_] = block[a, b]
        return carry

    def audio_pair(p, carry):
        tokens = audio[...].reshape(1024, 1024)
        lanes = pl.ds(pl.multiple_of(p * 256, 256), 256)
        more = pl.ds(pl.multiple_of(2048 + p * 256, 256), 256)
        kv[0] = dot(tokens, w_vmem[:, lanes]).astype(BF16)
        kv[1] = dot(tokens, w_vmem[:, more]).astype(BF16)
        for i in range(2):
            span = slice(i * 128, (i + 1) * 128)
            expo, total = softmax(dot_nt(q_heads[p * 2 + i], kv[0, :, span]))
            cross[p * 2 + i] = dot(expo.astype(BF16), kv[1, :, span]) * (1.0 / total)
        return carry

    wait(q_raw, local_sem.at[0])
    lax.fori_loop(0, CHUNKS, q_to_heads, 0)
    wait(k_raw, local_sem.at[1])
    lax.fori_loop(0, CHUNKS, k_to_heads, 0)

    wait(mine, aud_recv.at[0])
    theirs = audio.at[((x_hi + 1) % 2) * 4 + z, core]
    for d in (1, 3, 2):
        send(theirs, theirs, aud_send.at[0], aud_recv.at[1], at(x, y, (z + d) % 4, core))
    send_qkv(0, (2, 15))
    lax.fori_loop(0, 8, spatial_scores, 0)
    wait(earlier.at[:, 0], grad_recv.at[0])
    half = earlier.at[:, core]
    send(half, half, grad_send.at[5], grad_recv.at[5], at(x, y, z, 1 - core))
    send_qkv(1, (2, 15))
    wait(cotan, grad_recv.at[1])
    wait(earlier.at[:, 0], grad_recv.at[5])
    lax.fori_loop(0, 8, partial_rows, 0)

    right, left = (x + 1) % 4, (x + 3) % 4
    to_right, to_left = at(right, y, z, core), at(left, y, z, core)
    early, late = pl.ds(0, 2), pl.ds(2, 2)
    send(part_x.at[(x + 2) % 4, early], relay.at[0], grad_send.at[2], grad_recv.at[2], to_right)
    send(part_x.at[(x + 2) % 4, late], relay.at[1], grad_send.at[2], grad_recv.at[2], to_left)
    send(part_x.at[right, late], from_x.at[0, late], grad_send.at[2], grad_recv.at[6], to_right)
    send(part_x.at[left, early], from_x.at[1, early], grad_send.at[2], grad_recv.at[6], to_left)
    wait(audio_now, local_sem.at[3])
    wait(audio.at[pl.ds(0, 6), 0], aud_recv.at[1])
    side = audio.at[:, core]
    send(side, side, aud_send.at[1], aud_recv.at[2], at(x, y, z, 1 - core))
    send_qkv(2, (0, 15))
    temporal(0)
    wait(relay, grad_recv.at[2])
    merged[0] = (part_x[right, early].astype(F32) + relay[0].astype(F32)).astype(BF16)
    merged[1] = (part_x[left, late].astype(F32) + relay[1].astype(F32)).astype(BF16)
    send(merged.at[0], from_x.at[0, early], grad_send.at[6], grad_recv.at[6], to_right)
    send(merged.at[1], from_x.at[1, late], grad_send.at[6], grad_recv.at[6], to_left)
    wait(w_vmem, local_sem.at[2])
    wait(audio.at[:, 0], aud_recv.at[2])
    lax.fori_loop(0, 3, audio_pair, 0)
    temporal(1)
    send_qkv(3, (0, 15))
    lax.fori_loop(3, 6, audio_pair, 0)
    wait(from_x, grad_recv.at[6])
    for z_ in range(4):
        total = part_x[x, z_].astype(F32) + from_x[0, z_].astype(F32) + from_x[1, z_].astype(F32)
        part_z[z_] = total.astype(BF16)
    for d in (1, 3, 2):
        z_ = (z + d) % 4
        send(part_z.at[z_], from_z.at[z], grad_send.at[3], grad_recv.at[3], at(x, y, z_, core))
    local(part_z.at[z], from_z.at[z], grad_recv.at[3])

    temporal(2)
    lax.fori_loop(6, 8, audio_pair, 0)
    temporal(3)
    wait(from_z, grad_recv.at[3])
    for y_ in range(4):
        total = from_z[0, y_].astype(F32)
        for z_ in range(1, 4):
            total += from_z[z_, y_].astype(F32)
        part_y[y_] = total.reshape(2, 8, 512)
    cols = pl.ds(pl.multiple_of(line * 512, 512), 512)

    def send_rows(step, carry):
        y_, c_ = y_peer(step)
        send(part_y.at[y_, c_], rows.at[:, cols], grad_send.at[4], grad_recv.at[4], at(x, y_, z, c_))
        return carry

    lax.fori_loop(1, 8, send_rows, 0)
    local(part_y.at[y, core], rows.at[:, cols], grad_recv.at[4])

    for c in range(CHUNKS):
        wait(hidden.at[c], hid_recv.at[c])
        to_heads(hidden, hid_heads, c)

    def finish(i, carry):
        for h in [4 * i + j for j in range(4)]:
            values = hid_heads[h]
            result = values.astype(F32) + dot(spatial[h], values) + cross[h]
            out_heads[h] = result.astype(BF16)
        return carry

    lax.fori_loop(0, HEADS // 4, finish, 0)
    wait(rows, grad_recv.at[4])
    rows_out[...] = rows[...]

    for t, ref in enumerate((q_time, k_time, v_time)):
        wait(ref.at[pl.ds(0, 15)], qkv_send.at[t])
    wait(back.at[:, pl.ds(0, 15)], hid_send.at[0])
    wait(audio.at[pl.ds(0, 7), 0], aud_send.at[0])
    wait(audio.at[:, 0], aud_send.at[1])
    wait(earlier.at[pl.ds(0, 3), 0], grad_send.at[0])
    wait(earlier.at[:, 0], grad_send.at[5])
    wait(merged, grad_send.at[6])
    wait(cotan.at[pl.ds(0, 7)], grad_send.at[1])
    wait(from_x, grad_send.at[2])
    wait(from_z.at[pl.ds(0, 3)], grad_send.at[3])
    wait(rows.at[:, pl.ds(0, 7 * 512)], grad_send.at[4])


def permutation():
    row = lax.broadcasted_iota(jnp.int32, (256, 256), 0)
    col = lax.broadcasted_iota(jnp.int32, (256, 256), 1)
    return jnp.where(col == (row % 16) * 16 + row // 16, 1.0, 0.0).astype(BF16)


def write_out(out_heads, rows, mixed, grad, turned, sem):
    grad_copy = pltpu.make_async_copy(rows, grad, sem.at[0])
    grad_copy.start()
    perm = permutation()
    for c in range(CHUNKS):
        blocks = jnp.concatenate(
            [out_heads[:, c * 64 + i * 16 : c * 64 + (i + 1) * 16, :].reshape(256, HD) for i in range(4)],
            axis=1,
        )
        block = dot(perm, blocks).astype(BF16)
        for i in range(4):
            part = block[:, i * HD : (i + 1) * HD].reshape(16 // PART, PART, HEADS, HD)
            turned[c, pl.ds(i * (16 // PART), 16 // PART)] = part
        pltpu.make_async_copy(turned.at[c], mixed.at[:, c], sem.at[1]).start()
    pltpu.make_async_copy(turned, turned, sem.at[1]).wait()
    grad_copy.wait()


def local(
    q_time, k_time, v_time, q_space, k_space, audio_now, audio_earlier, cotangent, audio_weight
):
    split = (FRAMES, CHUNKS, PART, HEADS, HD)
    vmem = lambda shape, dtype: pltpu.VMEM(shape, dtype)
    dma = lambda n: pltpu.SemaphoreType.DMA((n,))
    anywhere = pl.BlockSpec(memory_space=pl.ANY)
    out_heads, rows = pl.pallas_call(
        kernel,
        out_shape=(
            jax.ShapeDtypeStruct((HEADS, SPOTS, HD), BF16),
            jax.ShapeDtypeStruct((8, 4096), F32),
        ),
        in_specs=[anywhere] * 9,
        out_specs=(pl.BlockSpec(memory_space=pltpu.VMEM),) * 2,
        scratch_shapes=[
            vmem((CHUNKS, 3, FRAMES, PART, HEADS, HD), BF16),
            vmem((CHUNKS, FRAMES, PART, HEADS, HD), BF16),
            vmem((CHUNKS, FRAMES, PART, HEADS, HD), BF16),
            vmem((CHUNKS, FRAMES, PART, HEADS, HD), BF16),
            vmem((CHUNKS, FRAMES, PART, HEADS, HD), BF16),
            vmem((HEADS, SPOTS, HD), BF16),
            vmem((HEADS, SPOTS, HD), BF16),
            vmem((HEADS, SPOTS, HD), BF16),
            vmem((HEADS, SPOTS, SPOTS), BF16),
            vmem((HEADS, SPOTS, HD), F32),
            vmem((8, 2, 64, 1024), BF16),
            vmem((1024, 4096), BF16),
            vmem((2, 1024, 256), BF16),
            vmem((4, 2, 64, 1024), BF16),
            vmem((8, 64, 512), BF16),
            vmem((4, 4, 4, 16, 512), BF16),
            vmem((2, 2, 4, 16, 512), BF16),
            vmem((2, 2, 4, 16, 512), BF16),
            vmem((2, 4, 4, 16, 512), BF16),
            vmem((4, 4, 16, 512), BF16),
            vmem((4, 4, 16, 512), BF16),
            vmem((4, 2, 8, 512), F32),
            vmem((8, 4096), F32),
            vmem((256, 256), F32),
            vmem((256, 256), BF16),
            dma(4), dma(3), dma(CHUNKS), dma(1), dma(CHUNKS), dma(2), dma(5), dma(7), dma(7),
        ],
        compiler_params=pltpu.CompilerParams(
            collective_id=0, has_side_effects=True, vmem_limit_bytes=LIMIT
        ),
        name="block",
    )(
        q_time.reshape(split), k_time.reshape(split), v_time.reshape(split),
        q_space.reshape(split), k_space.reshape(split),
        audio_now[0], audio_earlier[0], cotangent[0], audio_weight,
    )
    mixed, grad = pl.pallas_call(
        write_out,
        out_shape=(
            jax.ShapeDtypeStruct((FRAMES, CHUNKS, PART, HEADS, HD), BF16),
            jax.ShapeDtypeStruct((8, 4096), F32),
        ),
        in_specs=[pl.BlockSpec(memory_space=pltpu.VMEM)] * 2,
        out_specs=(anywhere, anywhere),
        scratch_shapes=[
            vmem((CHUNKS, FRAMES, PART, HEADS, HD), BF16),
            dma(2),
        ],
        compiler_params=pltpu.CompilerParams(vmem_limit_bytes=16 * 2**20),
        name="write_out",
    )(out_heads, rows)
    return mixed.reshape(1, 1, SPOTS, HEADS, HD), grad


def solution(mesh):
    placed = (
        P("dp", "seq", None, None, None),
        P("dp", "seq", None, None, None),
        P("dp", "seq", None, None, None),
        P("dp", "seq", None, None, None),
        P("dp", "seq", None, None, None),
        P("dp", "seq", None),
        P("dp", "seq", None),
        P("dp", "seq", None),
        P(),
    )
    return jax.shard_map(
        local,
        mesh=mesh,
        in_specs=placed,
        out_specs=(P("dp", "seq", None, None, None), P(("dp", "seq"), None)),
        check_vma=False,
    )
```

```python
import functools
import math

import jax
import jax.numpy as jnp
from jax import lax
from jax.experimental import pallas as pl
from jax.experimental.pallas import tpu as pltpu
from jax.sharding import PartitionSpec as P

MESH = pl.DeviceIdType.MESH
F32 = jnp.float32
BF16 = jnp.bfloat16
HEADS, HD, SPOTS, FRAMES = 16, 128, 256, 16
CHUNKS = 4
PART = SPOTS // FRAMES // CHUNKS
EXP_SCALE = math.log2(math.e) / math.sqrt(HD)
NEG = -1e30
LIMIT = 52 * 2**20


def dot(a, b):
    return lax.dot_general(a, b, (((1,), (0,)), ((), ())), preferred_element_type=F32)


def dot_nt(a, b):
    return lax.dot_general(a, b, (((1,), (1,)), ((), ())), preferred_element_type=F32)


def dot_tn(a, b):
    return lax.dot_general(a, b, (((0,), (0,)), ((), ())), preferred_element_type=F32)


def softmax(scores):
    row_max = jnp.max(scores, axis=-1, keepdims=True)
    expo = jnp.exp2((scores - row_max) * EXP_SCALE)
    return expo, jnp.sum(expo, axis=-1, keepdims=True)


def kernel(
    q_time, k_time, v_time, q_space, k_space, audio_now, audio_earlier, cotangent, weight,
    out_heads, rows_out,
    arrived, back, hidden, q_raw, k_raw, q_heads, k_heads, hid_heads, spatial, cross,
    audio, w_vmem, kv, earlier, cotan, part_x, relay, merged, from_x, part_z, from_z, part_y, rows, bias, perm,
    local_sem, qkv_send, qkv_recv, hid_send, hid_recv, aud_send, aud_recv, grad_send, grad_recv,
):
    dp = lax.axis_index("dp")
    me = lax.axis_index("seq")
    x_lo, y = dp // 4, dp % 4
    x_hi, z, core = me // 8, (me // 2) % 4, me % 2
    x = x_hi * 2 + x_lo
    line = y * 2 + core

    def at(x_, y_, z_, c_):
        return ((x_ % 2) * 4 + y_, (x_ // 2) * 8 + z_ * 2 + c_)

    def send(src, dst, send_sem, recv_sem, device):
        pltpu.make_async_remote_copy(
            src, dst, send_sem, recv_sem, device_id=device, device_id_type=MESH
        ).start()

    def local(src, dst, sem):
        pltpu.make_async_copy(src, dst, sem).start()

    def wait(ref, sem):
        pltpu.make_async_copy(ref, ref, sem).wait()

    def seq_peer(step):
        pure = 1 - (step + 14) // 16
        last = step // 14
        mid = 1 - pure - last
        far = pure + mid * (step % 2)
        along = mid * (1 + (step // 2 + 2) % 3)
        swap = pure * (step % 2) + mid * ((step + 4) // 6 % 2) + last
        return ((x_hi + far) % 2) * 8 + ((z + along) % 4) * 2 + (core + swap) % 2

    def y_peer(step):
        return (y + step // 2) % 4, (core + step) % 2

    barrier = pltpu.get_barrier_semaphore()

    def greet(device):
        pl.semaphore_signal(barrier, inc=1, device_id=device, device_id_type=MESH)

    def greet_seq(step, carry):
        greet((dp, (me + step) % 16))
        return carry

    lax.fori_loop(1, 16, greet_seq, 0)

    def greet_y(step, carry):
        y_, c_ = y_peer(step)
        greet(at(x, y_, z, c_))
        return carry

    lax.fori_loop(2, 8, greet_y, 0)
    greet(at((x + 1) % 4, y, z, core))
    greet(at((x + 3) % 4, y, z, core))
    pl.semaphore_wait(barrier, 23)

    mine = audio.at[me // 2, core]
    send(audio_now, mine, aud_send.at[0], aud_recv.at[0], at((x + 2) % 4, y, z, core))
    for d in (1, 3, 2):
        send(audio_now, mine, aud_send.at[0], aud_recv.at[1], at(x, y, (z + d) % 4, core))

    def send_qkv(c, steps):
        def one(peer):
            for t, ref in enumerate((q_time, k_time, v_time)):
                send(ref.at[peer, c], arrived.at[c, t, me], qkv_send.at[t], qkv_recv.at[c], (dp, peer))

        def body(step, carry):
            one(seq_peer(step))
            return carry

        lax.fori_loop(steps[0], steps[1], body, 0)

    send_qkv(0, (0, 2))
    send_qkv(1, (0, 2))
    send_qkv(2, (0, 2))
    send_qkv(3, (0, 2))
    def send_y(step, carry):
        y_, c_ = y_peer(step)
        to = at(x, y_, z, c_)
        cols = pl.ds(pl.multiple_of((y_ * 2 + c_) * 512, 512), 512)
        send(cotangent.at[:, cols], cotan.at[line], grad_send.at[1], grad_recv.at[1], to)
        return carry

    for d in (1, 3, 2):
        send(audio_earlier, earlier.at[y, core], grad_send.at[0], grad_recv.at[0], at(x, (y + d) % 4, z, core))
    lax.fori_loop(1, 8, send_y, 0)

    for c in range(CHUNKS):
        local(q_space.at[:, c], q_raw.at[c], local_sem.at[0])
        local(k_space.at[:, c], k_raw.at[c], local_sem.at[1])
        for t, ref in enumerate((q_time, k_time, v_time)):
            local(ref.at[me, c], arrived.at[c, t, me], qkv_recv.at[c])
    local(weight, w_vmem, local_sem.at[2])
    local(audio_now, audio.at[me // 2, core], local_sem.at[3])
    local(audio_earlier, earlier.at[y, core], grad_recv.at[0])
    local(cotangent.at[:, pl.ds(pl.multiple_of(line * 512, 512), 512)], cotan.at[line], grad_recv.at[1])

    row = lax.broadcasted_iota(jnp.int32, (256, 256), 0)
    col = lax.broadcasted_iota(jnp.int32, (256, 256), 1)
    bias[...] = jnp.where(row % 16 == col % 16, 0.0, NEG).astype(F32)
    perm[...] = permutation()

    def to_heads(src, dst, c):
        blocks = jnp.concatenate(
            [src[c, pl.ds(i * (16 // PART), 16 // PART)].reshape(256, HD) for i in range(4)], axis=1
        )
        turned = dot(perm[...], blocks).astype(BF16)
        for i in range(4):
            dst[:, pl.ds(pl.multiple_of(c * 64 + i * 16, 16), 16), :] = turned[
                :, i * HD : (i + 1) * HD
            ].reshape(HEADS, 16, HD)

    def q_to_heads(c, carry):
        to_heads(q_raw, q_heads, c)
        return carry

    def k_to_heads(c, carry):
        to_heads(k_raw, k_heads, c)
        return carry

    def spatial_scores(i, carry):
        for h in (2 * i, 2 * i + 1):
            expo, total = softmax(dot_nt(q_heads[h], k_heads[h]))
            spatial[h] = (expo * (1.0 / total)).astype(BF16)
        return carry

    def temporal(c):
        wait(arrived.at[c], qkv_recv.at[c])

        def attend(i, carry):
            for s in range(PART):
                queries = arrived[c, 0, :, s].reshape(256, HD)
                key_rows = arrived[c, 1, :, s].reshape(256, HD)
                values = arrived[c, 2, :, s].reshape(256, HD)
                expo, total = softmax(dot_nt(queries, key_rows) + bias[...])
                result = values.astype(F32) + dot(expo.astype(BF16), values) * (1.0 / total)
                back[c, :, s] = result.astype(BF16).reshape(FRAMES, HEADS, HD)
            return carry

        lax.fori_loop(0, 1, attend, 0)

        def go(step, carry):
            peer = seq_peer(step)
            send(back.at[c, peer], hidden.at[c, me], hid_send.at[0], hid_recv.at[c], (dp, peer))
            return carry

        lax.fori_loop(0, 15, go, 0)
        local(back.at[c, me], hidden.at[c, me], hid_recv.at[c])

    def partial_rows(i, carry):
        x_lo_, y_ = i // 4, i % 4
        lanes = pl.ds(pl.multiple_of(i * 128, 128), 128)
        block = dot_tn(earlier[:, :, :, lanes].reshape(512, 128), cotan[...].reshape(512, 512))
        block = block.astype(BF16).reshape(2, 4, 16, 512)
        for a in range(2):
            for b in range(4):
                part_x[a * 2 + x_lo_, b, y_] = block[a, b]
        return carry

    def audio_pair(p, carry):
        tokens = audio[...].reshape(1024, 1024)
        lanes = pl.ds(pl.multiple_of(p * 256, 256), 256)
        more = pl.ds(pl.multiple_of(2048 + p * 256, 256), 256)
        kv[0] = dot(tokens, w_vmem[:, lanes]).astype(BF16)
        kv[1] = dot(tokens, w_vmem[:, more]).astype(BF16)
        for i in range(2):
            span = slice(i * 128, (i + 1) * 128)
            expo, total = softmax(dot_nt(q_heads[p * 2 + i], kv[0, :, span]))
            cross[p * 2 + i] = dot(expo.astype(BF16), kv[1, :, span]) * (1.0 / total)
        return carry

    wait(q_raw, local_sem.at[0])
    lax.fori_loop(0, CHUNKS, q_to_heads, 0)
    wait(k_raw, local_sem.at[1])
    lax.fori_loop(0, CHUNKS, k_to_heads, 0)

    wait(mine, aud_recv.at[0])
    theirs = audio.at[((x_hi + 1) % 2) * 4 + z, core]
    for d in (1, 3, 2):
        send(theirs, theirs, aud_send.at[0], aud_recv.at[1], at(x, y, (z + d) % 4, core))
    send_qkv(0, (2, 15))
    lax.fori_loop(0, 8, spatial_scores, 0)
    wait(earlier.at[:, 0], grad_recv.at[0])
    half = earlier.at[:, core]
    send(half, half, grad_send.at[5], grad_recv.at[5], at(x, y, z, 1 - core))
    send_qkv(1, (2, 15))
    wait(cotan, grad_recv.at[1])
    wait(earlier.at[:, 0], grad_recv.at[5])
    lax.fori_loop(0, 8, partial_rows, 0)

    right, left = (x + 1) % 4, (x + 3) % 4
    to_right, to_left = at(right, y, z, core), at(left, y, z, core)
    early, late = pl.ds(0, 2), pl.ds(2, 2)
    send(part_x.at[(x + 2) % 4, early], relay.at[0], grad_send.at[2], grad_recv.at[2], to_right)
    send(part_x.at[(x + 2) % 4, late], relay.at[1], grad_send.at[2], grad_recv.at[2], to_left)
    send(part_x.at[right, late], from_x.at[0, late], grad_send.at[2], grad_recv.at[6], to_right)
    send(part_x.at[left, early], from_x.at[1, early], grad_send.at[2], grad_recv.at[6], to_left)
    send_qkv(2, (2, 15))
    wait(audio_now, local_sem.at[3])
    wait(audio.at[pl.ds(0, 6), 0], aud_recv.at[1])
    side = audio.at[:, core]
    send(side, side, aud_send.at[1], aud_recv.at[2], at(x, y, z, 1 - core))
    wait(w_vmem, local_sem.at[2])
    wait(audio.at[:, 0], aud_recv.at[2])
    lax.fori_loop(0, 2, audio_pair, 0)
    temporal(0)
    wait(relay, grad_recv.at[2])
    merged[0] = (part_x[right, early].astype(F32) + relay[0].astype(F32)).astype(BF16)
    merged[1] = (part_x[left, late].astype(F32) + relay[1].astype(F32)).astype(BF16)
    send(merged.at[0], from_x.at[0, early], grad_send.at[6], grad_recv.at[6], to_right)
    send(merged.at[1], from_x.at[1, late], grad_send.at[6], grad_recv.at[6], to_left)
    lax.fori_loop(2, 4, audio_pair, 0)
    send_qkv(3, (2, 8))
    temporal(1)
    send_qkv(3, (8, 15))
    lax.fori_loop(4, 6, audio_pair, 0)
    wait(from_x, grad_recv.at[6])
    for z_ in range(4):
        total = part_x[x, z_].astype(F32) + from_x[0, z_].astype(F32) + from_x[1, z_].astype(F32)
        part_z[z_] = total.astype(BF16)
    for d in (1, 3, 2):
        z_ = (z + d) % 4
        send(part_z.at[z_], from_z.at[z], grad_send.at[3], grad_recv.at[3], at(x, y, z_, core))
    local(part_z.at[z], from_z.at[z], grad_recv.at[3])

    temporal(2)
    lax.fori_loop(6, 8, audio_pair, 0)
    temporal(3)
    wait(from_z, grad_recv.at[3])
    for y_ in range(4):
        total = from_z[0, y_].astype(F32)
        for z_ in range(1, 4):
            total += from_z[z_, y_].astype(F32)
        part_y[y_] = total.reshape(2, 8, 512)
    cols = pl.ds(pl.multiple_of(line * 512, 512), 512)

    def send_rows(step, carry):
        y_, c_ = y_peer(step)
        send(part_y.at[y_, c_], rows.at[:, cols], grad_send.at[4], grad_recv.at[4], at(x, y_, z, c_))
        return carry

    lax.fori_loop(1, 8, send_rows, 0)
    local(part_y.at[y, core], rows.at[:, cols], grad_recv.at[4])

    for c in range(CHUNKS):
        wait(hidden.at[c], hid_recv.at[c])
        to_heads(hidden, hid_heads, c)

    def finish(i, carry):
        for h in [4 * i + j for j in range(4)]:
            values = hid_heads[h]
            result = values.astype(F32) + dot(spatial[h], values) + cross[h]
            out_heads[h] = result.astype(BF16)
        return carry

    lax.fori_loop(0, HEADS // 4, finish, 0)
    wait(rows, grad_recv.at[4])
    rows_out[...] = rows[...]

    for t, ref in enumerate((q_time, k_time, v_time)):
        wait(ref.at[pl.ds(0, 15)], qkv_send.at[t])
    wait(back.at[:, pl.ds(0, 15)], hid_send.at[0])
    wait(audio.at[pl.ds(0, 7), 0], aud_send.at[0])
    wait(audio.at[:, 0], aud_send.at[1])
    wait(earlier.at[pl.ds(0, 3), 0], grad_send.at[0])
    wait(earlier.at[:, 0], grad_send.at[5])
    wait(merged, grad_send.at[6])
    wait(cotan.at[pl.ds(0, 7)], grad_send.at[1])
    wait(from_x, grad_send.at[2])
    wait(from_z.at[pl.ds(0, 3)], grad_send.at[3])
    wait(rows.at[:, pl.ds(0, 7 * 512)], grad_send.at[4])


def permutation():
    row = lax.broadcasted_iota(jnp.int32, (256, 256), 0)
    col = lax.broadcasted_iota(jnp.int32, (256, 256), 1)
    return jnp.where(col == (row % 16) * 16 + row // 16, 1.0, 0.0).astype(BF16)


def write_out(out_heads, rows, mixed, grad, turned, sem):
    grad_copy = pltpu.make_async_copy(rows, grad, sem.at[0])
    grad_copy.start()
    perm = permutation()
    for c in range(CHUNKS):
        blocks = jnp.concatenate(
            [out_heads[:, c * 64 + i * 16 : c * 64 + (i + 1) * 16, :].reshape(256, HD) for i in range(4)],
            axis=1,
        )
        block = dot(perm, blocks).astype(BF16)
        for i in range(4):
            part = block[:, i * HD : (i + 1) * HD].reshape(16 // PART, PART, HEADS, HD)
            turned[c, pl.ds(i * (16 // PART), 16 // PART)] = part
        pltpu.make_async_copy(turned.at[c], mixed.at[:, c], sem.at[1]).start()
    pltpu.make_async_copy(turned, turned, sem.at[1]).wait()
    grad_copy.wait()


def local(
    q_time, k_time, v_time, q_space, k_space, audio_now, audio_earlier, cotangent, audio_weight
):
    split = (FRAMES, CHUNKS, PART, HEADS, HD)
    vmem = lambda shape, dtype: pltpu.VMEM(shape, dtype)
    dma = lambda n: pltpu.SemaphoreType.DMA((n,))
    anywhere = pl.BlockSpec(memory_space=pl.ANY)
    out_heads, rows = pl.pallas_call(
        kernel,
        out_shape=(
            jax.ShapeDtypeStruct((HEADS, SPOTS, HD), BF16),
            jax.ShapeDtypeStruct((8, 4096), F32),
        ),
        in_specs=[anywhere] * 9,
        out_specs=(pl.BlockSpec(memory_space=pltpu.VMEM),) * 2,
        scratch_shapes=[
            vmem((CHUNKS, 3, FRAMES, PART, HEADS, HD), BF16),
            vmem((CHUNKS, FRAMES, PART, HEADS, HD), BF16),
            vmem((CHUNKS, FRAMES, PART, HEADS, HD), BF16),
            vmem((CHUNKS, FRAMES, PART, HEADS, HD), BF16),
            vmem((CHUNKS, FRAMES, PART, HEADS, HD), BF16),
            vmem((HEADS, SPOTS, HD), BF16),
            vmem((HEADS, SPOTS, HD), BF16),
            vmem((HEADS, SPOTS, HD), BF16),
            vmem((HEADS, SPOTS, SPOTS), BF16),
            vmem((HEADS, SPOTS, HD), F32),
            vmem((8, 2, 64, 1024), BF16),
            vmem((1024, 4096), BF16),
            vmem((2, 1024, 256), BF16),
            vmem((4, 2, 64, 1024), BF16),
            vmem((8, 64, 512), BF16),
            vmem((4, 4, 4, 16, 512), BF16),
            vmem((2, 2, 4, 16, 512), BF16),
            vmem((2, 2, 4, 16, 512), BF16),
            vmem((2, 4, 4, 16, 512), BF16),
            vmem((4, 4, 16, 512), BF16),
            vmem((4, 4, 16, 512), BF16),
            vmem((4, 2, 8, 512), F32),
            vmem((8, 4096), F32),
            vmem((256, 256), F32),
            vmem((256, 256), BF16),
            dma(4), dma(3), dma(CHUNKS), dma(1), dma(CHUNKS), dma(2), dma(5), dma(7), dma(7),
        ],
        compiler_params=pltpu.CompilerParams(
            collective_id=0, has_side_effects=True, vmem_limit_bytes=LIMIT
        ),
        name="block",
    )(
        q_time.reshape(split), k_time.reshape(split), v_time.reshape(split),
        q_space.reshape(split), k_space.reshape(split),
        audio_now[0], audio_earlier[0], cotangent[0], audio_weight,
    )
    mixed, grad = pl.pallas_call(
        write_out,
        out_shape=(
            jax.ShapeDtypeStruct((FRAMES, CHUNKS, PART, HEADS, HD), BF16),
            jax.ShapeDtypeStruct((8, 4096), F32),
        ),
        in_specs=[pl.BlockSpec(memory_space=pltpu.VMEM)] * 2,
        out_specs=(anywhere, anywhere),
        scratch_shapes=[
            vmem((CHUNKS, FRAMES, PART, HEADS, HD), BF16),
            dma(2),
        ],
        compiler_params=pltpu.CompilerParams(vmem_limit_bytes=16 * 2**20),
        name="write_out",
    )(out_heads, rows)
    return mixed.reshape(1, 1, SPOTS, HEADS, HD), grad


def solution(mesh):
    placed = (
        P("dp", "seq", None, None, None),
        P("dp", "seq", None, None, None),
        P("dp", "seq", None, None, None),
        P("dp", "seq", None, None, None),
        P("dp", "seq", None, None, None),
        P("dp", "seq", None),
        P("dp", "seq", None),
        P("dp", "seq", None),
        P(),
    )
    return jax.shard_map(
        local,
        mesh=mesh,
        in_specs=placed,
        out_specs=(P("dp", "seq", None, None, None), P(("dp", "seq"), None)),
        check_vma=False,
    )
```
